32 devices in a mesh: wide: 8 (over y, x, core), narrow: 4 (over z).
Axes of the slice: x: 2, y: 2, z: 4, core: 2. Of those that a mesh axis runs over, the one named last changes fastest.
Arguments:
- tokens: bfloat16 [8192, 1024], P('wide', 'narrow'), may hold values from -6 to 6
- segments: int32 [8192], P('wide'), may hold values from 0 to 15, as said below
- first_gain: bfloat16 [1024], P('narrow'), may hold values from 0.25 to 1.75
- first_shift: bfloat16 [1024], P('narrow'), may hold values from -1.75 to 1.75
- qkv_weight: bfloat16 [1024, 3072], P('wide', 'narrow'), may hold values from -0.1875 to 0.1875
- qv_bias: bfloat16 [2048], P('narrow'), may hold values from -1.75 to 1.75
- dense_weight: bfloat16 [1024, 1024], P('narrow', 'wide'), may hold values from -0.5 to 0.5
- dense_bias: bfloat16 [1024], P('narrow'), may hold values from -1.75 to 1.75
- second_gain: bfloat16 [1024], P('narrow'), may hold values from 0.25 to 1.75
- second_shift: bfloat16 [1024], P('narrow'), may hold values from -1.75 to 1.75
- up_weight: bfloat16 [1024, 4096], P('wide', 'narrow'), may hold values from -0.1875 to 0.1875
- up_bias: bfloat16 [4096], P('narrow'), may hold values from -1.75 to 1.75
- down_weight: bfloat16 [4096, 1024], P('narrow', 'wide'), may hold values from -0.09375 to 0.09375
- down_bias: bfloat16 [1024], P('narrow'), may hold values from -1.75 to 1.75
- cotangent: bfloat16 [8192, 1024], P('wide', 'narrow'), may hold values from -8 to 8
Outputs:
- output: bfloat16 [8192, 1024], P('wide', 'narrow')
- token_grad: bfloat16 [8192, 1024], P('wide', 'narrow')
- first_gain_grad: float32 [1024], P('narrow')
- first_shift_grad: float32 [1024], P('narrow')
- qkv_weight_grad: float32 [1024, 3072], P('wide', 'narrow')
- qv_bias_grad: float32 [2048], P('narrow')
- dense_weight_grad: float32 [1024, 1024], P('narrow', 'wide')
- dense_bias_grad: float32 [1024], P('narrow')
- second_gain_grad: float32 [1024], P('narrow')
- second_shift_grad: float32 [1024], P('narrow')
- up_weight_grad: float32 [1024, 4096], P('wide', 'narrow')
- up_bias_grad: float32 [4096], P('narrow')
- down_weight_grad: float32 [4096, 1024], P('narrow', 'wide')
- down_bias_grad: float32 [1024], P('narrow')
The draws below stay inside these ranges and needn't reach their ends.
Inputs may be any that keep to these rules, and one draw needn't show every extreme that they name: `segments`: every aligned block b of 1024 positions holds either one whole sequence numbered 2 b, or two sequences of 512 positions numbered 2 b and 2 b + 1; the last block always holds two.
All inputs are finite; a program needn't handle non-finite values.
Results may differ from the reference program's by a relative error of at most 0.018.
Values may be sent and summed in bfloat16 or wider, within the bound.
A program may use at most 128 MiB of HBM per device.

```python
import jax
import jax.numpy as jnp
from jax import lax

D = 1024
H = 16
HD = 64
FF = 4096
TOK_DEV = 1024
TOKENS = 8192


def draw_segments(key, part):
    key = jax.random.fold_in(key, 7)
    block_count = TOKENS // TOK_DEV
    split_bits = jax.random.randint(key, (block_count, 1), 0, 2)
    last_block = (jnp.arange(block_count)[:, None] == block_count - 1).astype(jnp.int32)
    split_bits = jnp.maximum(split_bits, last_block)
    positions = jnp.arange(TOK_DEV)[None, :]
    first_ids = 2 * jnp.arange(block_count)[:, None]
    second_half = (positions >= TOK_DEV // 2).astype(jnp.int32)
    return (first_ids + split_bits * second_half).reshape(TOKENS).astype(jnp.int32)


def with_spikes(values, own_key, source, target, parts, factor):
    owner, partner = [(jnp.arange(values.shape[dim]) // (values.shape[dim] // parts)).reshape([-1 if axis == dim else 1 for axis in range(values.ndim)]) for dim in (source, target)]
    chosen = jax.random.permutation(own_key, parts)[partner]
    strong = (owner == chosen) | (owner == (partner + parts // 2) % parts)
    return jnp.where(strong, factor * values, values)


def level_of(stream_key, extent, cuts, least, largest):
    level = 1.0
    for axis_at, blocks in cuts:
        heights = jax.random.uniform(jax.random.fold_in(jax.random.fold_in(stream_key, 6), axis_at), (blocks,), jnp.float32, least / len(cuts), largest / len(cuts))
        level = level * jnp.repeat(jnp.exp(heights), extent[axis_at] // blocks).reshape((-1,) + (1,) * (len(extent) - 1 - axis_at))
    return level


def gaussian(stream_key, extent, scale, bound, shards=(), dtype=jnp.bfloat16):
    factor_of = level_of(stream_key, extent, shards, -0.22, 0.18) if shards else 1.0
    drawn = jax.random.normal(stream_key, extent, jnp.float32) * scale * factor_of
    return jnp.minimum(jnp.maximum(drawn, -bound), bound).astype(dtype)


def noise_with(stream_key, extent, spread, reach, pieces, heavy, dtype=jnp.bfloat16):
    array = spread * jax.random.normal(stream_key, extent, jnp.float32)
    if pieces:
        array = array * level_of(stream_key, extent, pieces, -0.22, 0.18)
    return jnp.clip(with_spikes(array, jax.random.fold_in(stream_key, 3), *heavy), -reach, reach).astype(dtype)


def setup_inputs(seed: int = 0) -> dict:
    seeds = jax.random.split(jax.random.key(seed), 16)
    tokens = gaussian(seeds[0], (TOKENS, D), 1.0, 6.0, ((0, 8), (1, 4)))
    segments = draw_segments(jax.random.fold_in(seeds[15], 71), 0)
    first_gain = jnp.clip(1.0 + 0.15 * jax.random.normal(seeds[2], (D,), jnp.float32), 0.25, 1.75).astype(jnp.bfloat16)
    first_shift = gaussian(seeds[3], (D,), 0.3, 1.75, ((0, 4),))
    qkv_weight = gaussian(seeds[4], (D, 3 * D), D ** -0.5, 0.1875, ((0, 8), (1, 4)))
    qv_bias = gaussian(seeds[5], (2 * D,), 0.3, 1.75, ((0, 4),))
    dense_weight = gaussian(seeds[6], (D, D), (D // 8) ** -0.5, 0.5, ((0, 4), (1, 8)))
    dense_bias = gaussian(seeds[7], (D,), 0.3, 1.75, ((0, 4),))
    second_gain = jnp.clip(1.0 + 0.15 * jax.random.normal(seeds[8], (D,), jnp.float32), 0.25, 1.75).astype(jnp.bfloat16)
    second_shift = gaussian(seeds[9], (D,), 0.3, 1.75, ((0, 4),))
    up_weight = gaussian(seeds[10], (D, FF), D ** -0.5, 0.1875, ((0, 8), (1, 4)))
    up_bias = gaussian(seeds[11], (FF,), 0.3, 1.75, ((0, 4),))
    down_weight = gaussian(seeds[12], (FF, D), FF ** -0.5, 0.09375, ((0, 4), (1, 8)))
    down_bias = gaussian(seeds[13], (D,), 0.3, 1.75, ((0, 4),))
    cotangent = noise_with(seeds[14], (TOKENS, D), 1.0, 8.0, ((0, 8), (1, 4)), (0, 1, 8, 2.0))
    return {"tokens": tokens, "segments": segments, "first_gain": first_gain, "first_shift": first_shift, "qkv_weight": qkv_weight, "qv_bias": qv_bias, "dense_weight": dense_weight, "dense_bias": dense_bias, "second_gain": second_gain, "second_shift": second_shift, "up_weight": up_weight, "up_bias": up_bias, "down_weight": down_weight, "down_bias": down_bias, "cotangent": cotangent}


eps = 1e-05
negative = -1e+30
highest = lax.Precision.HIGHEST

@jax.custom_vjp
def low(v):
    return lax.optimization_barrier(v.astype(jnp.bfloat16)).astype(jnp.float32)

@jax.custom_vjp
def low_back(v):
    return v

def low_keep(v):
    return (low(v), None)

def low_pass(kept, grad):
    return (grad,)

def back_keep(v):
    return (v, None)

def back_low(kept, grad):
    return (low(grad),)
low.defvjp(low_keep, low_pass)
low_back.defvjp(back_keep, back_low)

def normalize(values, gain, shift):
    mean_value = lax.optimization_barrier(jnp.mean(values, axis=-1, keepdims=True))
    centered = values - mean_value
    inv_std = lax.rsqrt(lax.optimization_barrier(jnp.mean(centered * centered, axis=-1, keepdims=True)) + eps)
    return centered * inv_std * gain + shift

def block_layer(params, tok_block, seg_block):
    first_gain, first_shift, qkv_weight, qv_bias, dense_weight, dense_bias, second_gain, second_shift, up_weight, up_bias, down_weight, down_bias = params
    length = tok_block.shape[0]
    act_one = low(normalize(tok_block, first_gain, first_shift))
    projected = jnp.dot(act_one, qkv_weight, precision=highest).reshape(length, H, 3, HD)
    bias_pair = qv_bias.reshape(H, 2, HD)
    zero_part = jnp.zeros((H, HD), jnp.float32)
    full_bias = jnp.stack([bias_pair[:, 0], zero_part, bias_pair[:, 1]], axis=1)
    projected = low_back(low(projected + full_bias[None]))
    query = projected[:, :, 0]
    keys = projected[:, :, 1]
    values = projected[:, :, 2]
    positions = jnp.arange(length)
    distance = (positions[:, None] - positions[None, :]).astype(jnp.float32)
    slopes = 2.0 ** (-8.0 * (jnp.arange(H) + 1).astype(jnp.float32) / H)
    scores = jnp.einsum('qhd,khd->hqk', query, keys, precision=highest) * HD ** (-0.5)
    scores = low_back(scores - slopes[:, None, None] * distance[None])
    allowed = (positions[None, :] <= positions[:, None]) & (seg_block[:, None] == seg_block[None, :])
    scores = jnp.where(allowed[None], scores, negative)
    top_score = lax.optimization_barrier(jnp.max(scores, axis=-1, keepdims=True))
    exponent = jnp.exp(scores - top_score)
    weights = low(exponent / lax.optimization_barrier(jnp.sum(exponent, axis=-1, keepdims=True)))
    attended = jnp.einsum('hqk,khd->qhd', weights, values, precision=highest).reshape(length, H * HD)
    attended = low_back(low(attended))
    mixed = low_back(jnp.dot(attended, dense_weight, precision=highest) + dense_bias)
    residual = tok_block + mixed
    act_two = low(normalize(residual, second_gain, second_shift))
    pre_act = low_back(jnp.dot(act_two, up_weight, precision=highest) + up_bias)
    hidden = low(jax.nn.gelu(pre_act, approximate=True))
    return residual + low_back(jnp.dot(hidden, down_weight, precision=highest) + down_bias)

def reference(tokens, segments, first_gain, first_shift, qkv_weight, qv_bias, dense_weight, dense_bias, second_gain, second_shift, up_weight, up_bias, down_weight, down_bias, cotangent):
    params = tuple((item.astype(jnp.float32) for item in (first_gain, first_shift, qkv_weight, qv_bias, dense_weight, dense_bias, second_gain, second_shift, up_weight, up_bias, down_weight, down_bias)))
    seg_blocks = segments.reshape(-1, TOK_DEV)

    def forward(weights_all, inputs):
        tok_blocks = inputs.reshape(-1, TOK_DEV, D)
        stepper = jax.checkpoint(lambda pair: block_layer(weights_all, pair[0], pair[1]))
        return lax.map(stepper, (tok_blocks, seg_blocks)).reshape(-1, D)
    result, pullback = jax.vjp(forward, params, tokens.astype(jnp.float32))
    param_grads, token_grad = pullback(cotangent.astype(jnp.float32))
    g_first_gain, g_first_shift, g_qkv_weight, g_qv_bias, g_dense_weight, g_dense_bias, g_second_gain, g_second_shift, g_up_weight, g_up_bias, g_down_weight, g_down_bias = param_grads
    return (result.astype(jnp.bfloat16), token_grad.astype(jnp.bfloat16), g_first_gain, g_first_shift, g_qkv_weight, g_qv_bias, g_dense_weight, g_dense_bias, g_second_gain, g_second_shift, g_up_weight, g_up_bias, g_down_weight, g_down_bias)
```

```python
from functools import partial

import jax
import jax.numpy as jnp
from jax import lax
from jax.experimental import pallas as pl
from jax.experimental.pallas import tpu as pltpu
from jax.sharding import PartitionSpec as P

H = 16
HD = 64


eps = 1e-05
negative = -1e30
block_rows = 256
head_group = 2


def normalize(values, gain, shift):
    mean_value = jnp.mean(values, axis=-1, keepdims=True)
    centered = values - mean_value
    inv_std = lax.rsqrt(jnp.mean(centered * centered, axis=-1, keepdims=True) + eps)
    normed = centered * inv_std
    return (normed * gain + shift, normed, inv_std)


def norm_backward(grad_norm, gain, normed, inv_std):
    scaled = grad_norm * gain
    mean_one = jnp.mean(scaled, axis=-1, keepdims=True)
    mean_two = jnp.mean(scaled * normed, axis=-1, keepdims=True)
    return inv_std * (scaled - mean_one - normed * mean_two)


def own_columns(values, col_start, local_width):
    return lax.dynamic_slice_in_dim(values, col_start, local_width, values.ndim - 1)


def contract(left, right, left_dim, right_dim):
    return lax.dot_general(
        left, right, (((left_dim,), (right_dim,)), ((), ())), preferred_element_type=jnp.float32
    )


def score_block(seg_ref, query_block, keys, slope, row_start, tok_rows):
    row_end = keys.shape[0]
    logits = contract(keys, query_block, 1, 1)
    key_pos = lax.broadcasted_iota(jnp.int32, (row_end, 1), 0)
    query_pos = row_start + lax.broadcasted_iota(jnp.int32, (1, query_block.shape[0]), 1)
    half = tok_rows // 2
    shared = (seg_ref[0] == seg_ref[half]).astype(jnp.int32)
    first_key = 0 if row_start < half else jnp.where(shared == 1, 0, half)
    key_term = slope * (key_pos - row_start).astype(jnp.float32)
    allowed = (key_pos <= query_pos) & (key_pos >= first_key)
    return jnp.where(allowed, logits + key_term, negative)


def forward_body(seg_ref, slope_ref, packed_ref, out_ref, total_ref):
    tok_rows = packed_ref.shape[0]
    group = pl.program_id(0)
    for item in range(head_group):
        slope = slope_ref[group * head_group + item]
        base = item * 3 * HD
        for row_start in range(0, tok_rows, block_rows):
            row_end = row_start + block_rows
            rows = slice(row_start, row_end)
            query = packed_ref[rows, base : base + HD] * jnp.bfloat16(HD ** (-0.5))
            keys = packed_ref[:row_end, base + HD : base + 2 * HD]
            values = packed_ref[:row_end, base + 2 * HD : base + 3 * HD]
            logits = score_block(seg_ref, query, keys, slope, row_start, tok_rows)
            top = jnp.max(logits, axis=0, keepdims=True)
            powers = jnp.exp(logits - top)
            total = jnp.sum(powers, axis=0, keepdims=True)
            probs = (powers * (1.0 / total)).astype(jnp.bfloat16)
            result = contract(values, probs, 0, 0)
            out_ref[rows, item * HD : (item + 1) * HD] = result.T.astype(jnp.bfloat16)
            total_ref[0, item : item + 1, rows] = top + jnp.log(total)


def backward_body(seg_ref, slope_ref, packed_ref, total_ref, grad_ref, out_ref, key_sum, value_sum):
    tok_rows = packed_ref.shape[0]
    group = pl.program_id(0)
    scale = HD ** (-0.5)
    for item in range(head_group):
        slope = slope_ref[group * head_group + item]
        base = item * 3 * HD
        for row_start in reversed(range(0, tok_rows, block_rows)):
            row_end = row_start + block_rows
            rows = slice(row_start, row_end)
            query = packed_ref[rows, base : base + HD] * jnp.bfloat16(scale)
            keys = packed_ref[:row_end, base + HD : base + 2 * HD]
            values = packed_ref[:row_end, base + 2 * HD : base + 3 * HD]
            grad = grad_ref[rows, item * HD : (item + 1) * HD]
            logits = score_block(seg_ref, query, keys, slope, row_start, tok_rows)
            probs = jnp.exp(logits - total_ref[0, item : item + 1, rows])
            grad_probs = contract(values, grad, 1, 1)
            weighted = jnp.sum(probs * grad_probs, axis=0, keepdims=True)
            grad_logits = (probs * (grad_probs - weighted)).astype(jnp.bfloat16)
            grad_query = contract(keys, grad_logits, 0, 0) * scale
            out_ref[rows, base : base + HD] = grad_query.T.astype(jnp.bfloat16)
            grad_key = contract(grad_logits, query, 1, 0)
            grad_value = contract(probs.astype(jnp.bfloat16), grad, 1, 0)
            if row_end == tok_rows:
                key_sum[...] = grad_key
                value_sum[...] = grad_value
            else:
                key_sum[:row_end, :] += grad_key
                value_sum[:row_end, :] += grad_value
        out_ref[:, base + HD : base + 2 * HD] = key_sum[...].astype(jnp.bfloat16)
        out_ref[:, base + 2 * HD : base + 3 * HD] = value_sum[...].astype(jnp.bfloat16)


def attend_specs(tok_rows):
    scalars = pl.BlockSpec(memory_space=pltpu.SMEM)
    packed = pl.BlockSpec((tok_rows, head_group * 3 * HD), lambda g: (0, g))
    totals = pl.BlockSpec((1, head_group, tok_rows), lambda g: (g, 0, 0))
    heads = pl.BlockSpec((tok_rows, head_group * HD), lambda g: (0, g))
    return scalars, packed, totals, heads


def attend_forward(packed, slopes, segments):
    tok_rows, width = packed.shape
    heads_here = width // (3 * HD)
    groups = heads_here // head_group
    scalars, packed_spec, totals, heads = attend_specs(tok_rows)
    return pl.pallas_call(
        forward_body,
        grid=(groups,),
        in_specs=[scalars, scalars, packed_spec],
        out_specs=[heads, totals],
        out_shape=[
            jax.ShapeDtypeStruct((tok_rows, heads_here * HD), jnp.bfloat16),
            jax.ShapeDtypeStruct((groups, head_group, tok_rows), jnp.float32),
        ],
        compiler_params=pltpu.CompilerParams(vmem_limit_bytes=40 * 2**20),
        cost_estimate=pl.CostEstimate(
            flops=4 * heads_here * tok_rows * tok_rows * HD,
            bytes_accessed=2 * tok_rows * width * 2,
            transcendentals=heads_here * tok_rows * tok_rows,
        ),
    )(segments, slopes, packed)


def attend_backward(packed, slopes, segments, log_totals, grad_attended):
    tok_rows, width = packed.shape
    heads_here = width // (3 * HD)
    scalars, packed_spec, totals, heads = attend_specs(tok_rows)
    return pl.pallas_call(
        backward_body,
        grid=(heads_here // head_group,),
        in_specs=[scalars, scalars, packed_spec, totals, heads],
        out_specs=packed_spec,
        out_shape=jax.ShapeDtypeStruct((tok_rows, width), jnp.bfloat16),
        scratch_shapes=[
            pltpu.VMEM((tok_rows, HD), jnp.float32),
            pltpu.VMEM((tok_rows, HD), jnp.float32),
        ],
        compiler_params=pltpu.CompilerParams(vmem_limit_bytes=40 * 2**20),
        cost_estimate=pl.CostEstimate(
            flops=10 * heads_here * tok_rows * tok_rows * HD,
            bytes_accessed=3 * tok_rows * width * 2,
            transcendentals=heads_here * tok_rows * tok_rows,
        ),
    )(segments, slopes, packed, log_totals, grad_attended)


def exchange_body(scatter, count, devices, *refs):
    sources, results = refs[:count], refs[count : 2 * count]
    local_sem, send_sem, recv_sem = refs[2 * count :]
    me = lax.axis_index("wide")

    barrier = pltpu.get_barrier_semaphore()

    def greet(step, carry):
        peer = lax.rem(me + step, devices)
        pl.semaphore_signal(
            barrier, inc=1, device_id={"wide": peer}, device_id_type=pl.DeviceIdType.MESH
        )
        return carry

    lax.fori_loop(1, devices, greet, 0)
    pl.semaphore_wait(barrier, devices - 1)

    def block_of(item, owner):
        return sources[item].at[owner] if scatter else sources[item]

    def copy_to(item, step):
        peer = lax.rem(me + step, devices)
        return pltpu.make_async_remote_copy(
            src_ref=block_of(item, peer),
            dst_ref=results[item].at[me],
            send_sem=send_sem.at[item, step],
            recv_sem=recv_sem.at[item, step],
            device_id={"wide": peer},
            device_id_type=pl.DeviceIdType.MESH,
        )

    def own_copy(item):
        return pltpu.make_async_copy(
            block_of(item, me), results[item].at[me], local_sem.at[item]
        )

    def start(step, carry):
        for item in range(count):
            copy_to(item, step).start()
        return carry

    def finish(step, carry):
        for item in range(count):
            copy_to(item, step).wait()
        return carry

    lax.fori_loop(1, devices, start, 0)
    for item in range(count):
        own_copy(item).start()
    for item in range(count):
        own_copy(item).wait()
    lax.fori_loop(1, devices, finish, 0)


def exchange(sources, scatter, call_id):
    devices = lax.axis_size("wide")
    count = len(sources)
    shapes = [item.shape[1:] if scatter else item.shape for item in sources]
    size = sum(devices * rows * width * 2 for rows, width in shapes)
    return pl.pallas_call(
        partial(exchange_body, scatter, count, devices),
        in_specs=[pl.BlockSpec(memory_space=pl.ANY)] * count,
        out_specs=[pl.BlockSpec(memory_space=pl.ANY)] * count,
        out_shape=[
            jax.ShapeDtypeStruct((devices, *shape), item.dtype)
            for shape, item in zip(shapes, sources)
        ],
        scratch_shapes=[
            pltpu.SemaphoreType.DMA((count,)),
            pltpu.SemaphoreType.DMA((count, devices)),
            pltpu.SemaphoreType.DMA((count, devices)),
        ],
        compiler_params=pltpu.CompilerParams(collective_id=call_id, has_side_effects=True),
        cost_estimate=pl.CostEstimate(flops=0, bytes_accessed=20 * size, transcendentals=0),
    )(*sources)


def gather_rows(sources, call_id):
    return [
        item.reshape(-1, item.shape[-1]) for item in exchange(sources, False, call_id)
    ]


def scatter_sums(sources, call_id):
    devices = lax.axis_size("wide")
    blocks = [item.reshape(devices, -1, item.shape[-1]) for item in sources]
    return [
        jnp.sum(item.astype(jnp.float32), axis=0) for item in exchange(blocks, True, call_id)
    ]


def local(
    tokens,
    segments,
    first_gain,
    first_shift,
    qkv_weight,
    qv_bias,
    dense_weight,
    dense_bias,
    second_gain,
    second_shift,
    up_weight,
    up_bias,
    down_weight,
    down_bias,
    cotangent,
):
    tok_rows, local_width = tokens.shape
    col_start = lax.axis_index("narrow") * local_width
    heads_here = qv_bias.shape[0] // (2 * HD)
    head_first = lax.axis_index("narrow") * heads_here
    slopes = 2.0 ** (-8.0 * (head_first + jnp.arange(heads_here) + 1).astype(jnp.float32) / H)
    out_rows = dense_weight.shape[1]
    vectors = jnp.stack([first_gain, first_shift, dense_bias, second_gain, second_shift])
    vectors = jnp.pad(vectors, ((0, 11), (0, 0)))
    joined = lax.all_gather(
        jnp.concatenate([tokens, dense_weight.T, vectors], axis=0), "narrow", axis=1, tiled=True
    )
    full_tokens = joined[:tok_rows]
    dense_block = joined[tok_rows : tok_rows + out_rows]
    gain_one, shift_one, bias_dense, gain_two, shift_two = (
        joined[tok_rows + out_rows + item].astype(jnp.float32) for item in range(5)
    )
    qkv_full, up_full = gather_rows([qkv_weight, up_weight], 0)
    grad_out = lax.all_gather(cotangent, "narrow", axis=1, tiled=True)
    inputs = full_tokens.astype(jnp.float32)
    normed_one, hat_one, inv_one = normalize(inputs, gain_one, shift_one)
    act_one = normed_one.astype(jnp.bfloat16)
    bias_pair = qv_bias.astype(jnp.float32).reshape(heads_here, 2, HD)
    full_bias = jnp.stack(
        [bias_pair[:, 0], jnp.zeros_like(bias_pair[:, 0]), bias_pair[:, 1]], axis=1
    ).reshape(-1)
    packed = (
        jnp.dot(act_one, qkv_full, preferred_element_type=jnp.float32) + full_bias[None]
    ).astype(jnp.bfloat16)
    attended, log_totals = attend_forward(packed, slopes, segments)
    attended_full = lax.all_gather(attended, "narrow", axis=1, tiled=True)
    dense_rows, down_rows = gather_rows([dense_block, down_weight.T], 1)
    mixed = contract(attended_full, dense_rows, 1, 1)
    residual = inputs + (mixed + bias_dense)
    normed_two, hat_two, inv_two = normalize(residual, gain_two, shift_two)
    act_two = normed_two.astype(jnp.bfloat16)
    pre_act = jnp.dot(act_two, up_full, preferred_element_type=jnp.float32) + up_bias.astype(
        jnp.float32
    )
    hidden = jax.nn.gelu(pre_act, approximate=True).astype(jnp.bfloat16)
    grad_hidden = jnp.dot(grad_out, down_rows, preferred_element_type=jnp.float32)
    _, gelu_back = jax.vjp(partial(jax.nn.gelu, approximate=True), pre_act)
    grad_pre = gelu_back(grad_hidden)[0].astype(jnp.bfloat16)
    grad_act_two = lax.psum(
        contract(grad_pre, up_full, 1, 1).astype(jnp.bfloat16), "narrow"
    ).astype(jnp.float32)
    mlp_out = lax.psum_scatter(
        contract(hidden, down_rows, 1, 1).astype(jnp.bfloat16),
        "narrow",
        scatter_dimension=1,
        tiled=True,
    ).astype(jnp.float32)
    output = (
        own_columns(residual, col_start, local_width) + (mlp_out + down_bias.astype(jnp.float32))
    ).astype(jnp.bfloat16)
    down_bias_grad = jnp.sum(cotangent.astype(jnp.float32), axis=0)
    up_bias_grad = jnp.sum(grad_pre.astype(jnp.float32), axis=0)
    grad_down = contract(grad_out, hidden, 0, 0).astype(jnp.bfloat16)
    grad_up = contract(act_two, grad_pre, 0, 0).astype(jnp.bfloat16)
    up_weight_grad, down_rows_grad = scatter_sums([grad_up, grad_down], 2)
    second_gain_grad = own_columns(jnp.sum(grad_act_two * hat_two, axis=0), col_start, local_width)
    second_shift_grad = own_columns(jnp.sum(grad_act_two, axis=0), col_start, local_width)
    grad_residual = grad_out.astype(jnp.float32) + norm_backward(
        grad_act_two, gain_two, hat_two, inv_two
    )
    grad_branch = grad_residual.astype(jnp.bfloat16)
    dense_bias_grad = own_columns(
        jnp.sum(grad_branch.astype(jnp.float32), axis=0), col_start, local_width
    )
    grad_attended = jnp.dot(
        grad_branch,
        own_columns(dense_rows, col_start, local_width),
        preferred_element_type=jnp.float32,
    ).astype(jnp.bfloat16)
    grad_packed = attend_backward(packed, slopes, segments, log_totals, grad_attended)
    column_sums = jnp.sum(grad_packed.astype(jnp.float32), axis=0).reshape(heads_here, 3, HD)
    qv_bias_grad = jnp.stack([column_sums[:, 0], column_sums[:, 2]], axis=1).reshape(-1)
    grad_one_part = contract(grad_packed, qkv_full, 1, 1)
    grad_act_one = lax.psum_scatter(
        grad_one_part.astype(jnp.bfloat16), "narrow", scatter_dimension=1, tiled=True
    ).astype(jnp.float32)
    scaled_part = grad_one_part * gain_one
    sum_plain, sum_hat, gain_part, shift_part = lax.psum(
        (
            jnp.sum(scaled_part, axis=1),
            jnp.sum(scaled_part * hat_one, axis=1),
            jnp.sum(grad_one_part * hat_one, axis=0),
            jnp.sum(grad_one_part, axis=0),
        ),
        "narrow",
    )
    grad_qkv = contract(act_one, grad_packed, 0, 0).astype(jnp.bfloat16)
    grad_dense = contract(grad_branch, attended, 0, 0).astype(jnp.bfloat16)
    qkv_weight_grad, dense_rows_grad = scatter_sums([grad_qkv, grad_dense], 3)
    small = (
        own_columns(gain_part, col_start, local_width),
        own_columns(shift_part, col_start, local_width),
        qv_bias_grad,
        dense_bias_grad,
        second_gain_grad,
        second_shift_grad,
        up_bias_grad,
        down_bias_grad,
    )
    small_sums = lax.psum(jnp.concatenate(small), "wide")
    bounds = [0]
    for item in small:
        bounds.append(bounds[-1] + item.shape[0])
    (
        first_gain_grad,
        first_shift_grad,
        qv_bias_grad,
        dense_bias_grad,
        second_gain_grad,
        second_shift_grad,
        up_bias_grad,
        down_bias_grad,
    ) = (small_sums[low:high] for low, high in zip(bounds, bounds[1:]))
    hat_local = own_columns(hat_one, col_start, local_width)
    scaled = grad_act_one * first_gain.astype(jnp.float32)
    full_width = local_width * lax.axis_size("narrow")
    grad_norm_one = inv_one * (
        scaled - sum_plain[:, None] / full_width - hat_local * sum_hat[:, None] / full_width
    )
    token_grad = (own_columns(grad_residual, col_start, local_width) + grad_norm_one).astype(
        jnp.bfloat16
    )
    dense_weight_grad = dense_rows_grad.T
    down_weight_grad = down_rows_grad.T
    return (
        output,
        token_grad,
        first_gain_grad,
        first_shift_grad,
        qkv_weight_grad,
        qv_bias_grad,
        dense_weight_grad,
        dense_bias_grad,
        second_gain_grad,
        second_shift_grad,
        up_weight_grad,
        up_bias_grad,
        down_weight_grad,
        down_bias_grad,
    )


def solution(mesh):
    in_specs = (
        P("wide", "narrow"),
        P("wide"),
        P("narrow"),
        P("narrow"),
        P("wide", "narrow"),
        P("narrow"),
        P("narrow", "wide"),
        P("narrow"),
        P("narrow"),
        P("narrow"),
        P("wide", "narrow"),
        P("narrow"),
        P("narrow", "wide"),
        P("narrow"),
        P("wide", "narrow"),
    )
    out_specs = (
        P("wide", "narrow"),
        P("wide", "narrow"),
        P("narrow"),
        P("narrow"),
        P("wide", "narrow"),
        P("narrow"),
        P("narrow", "wide"),
        P("narrow"),
        P("narrow"),
        P("narrow"),
        P("wide", "narrow"),
        P("narrow"),
        P("narrow", "wide"),
        P("narrow"),
    )
    return jax.shard_map(local, mesh=mesh, in_specs=in_specs, out_specs=out_specs, check_vma=False)
```

```python
from functools import partial

import jax
import jax.numpy as jnp
from jax import lax
from jax.experimental import pallas as pl
from jax.experimental.pallas import tpu as pltpu
from jax.sharding import PartitionSpec as P

H = 16
HD = 64


eps = 1e-05
negative = -1e30
block_rows = 256
head_group = 2


def normalize(values, gain, shift):
    mean_value = jnp.mean(values, axis=-1, keepdims=True)
    centered = values - mean_value
    inv_std = lax.rsqrt(jnp.mean(centered * centered, axis=-1, keepdims=True) + eps)
    normed = centered * inv_std
    return (normed * gain + shift, normed, inv_std)


def norm_backward(grad_norm, gain, normed, inv_std):
    scaled = grad_norm * gain
    mean_one = jnp.mean(scaled, axis=-1, keepdims=True)
    mean_two = jnp.mean(scaled * normed, axis=-1, keepdims=True)
    return inv_std * (scaled - mean_one - normed * mean_two)


def own_columns(values, col_start, local_width):
    return lax.dynamic_slice_in_dim(values, col_start, local_width, values.ndim - 1)


def contract(left, right, left_dim, right_dim):
    return lax.dot_general(
        left, right, (((left_dim,), (right_dim,)), ((), ())), preferred_element_type=jnp.float32
    )


def score_block(seg_ref, query_block, keys, slope, row_start, tok_rows):
    row_end = keys.shape[0]
    logits = contract(keys, query_block, 1, 1)
    key_pos = lax.broadcasted_iota(jnp.int32, (row_end, 1), 0)
    query_pos = row_start + lax.broadcasted_iota(jnp.int32, (1, query_block.shape[0]), 1)
    half = tok_rows // 2
    shared = (seg_ref[0] == seg_ref[half]).astype(jnp.int32)
    first_key = 0 if row_start < half else jnp.where(shared == 1, 0, half)
    key_term = slope * (key_pos - row_start).astype(jnp.float32)
    allowed = (key_pos <= query_pos) & (key_pos >= first_key)
    return jnp.where(allowed, logits + key_term, negative)


def forward_body(seg_ref, slope_ref, packed_ref, out_ref, total_ref):
    tok_rows = packed_ref.shape[0]
    group = pl.program_id(0)
    for item in range(head_group):
        slope = slope_ref[group * head_group + item]
        base = item * 3 * HD
        for row_start in range(0, tok_rows, block_rows):
            row_end = row_start + block_rows
            rows = slice(row_start, row_end)
            query = packed_ref[rows, base : base + HD] * jnp.bfloat16(HD ** (-0.5))
            keys = packed_ref[:row_end, base + HD : base + 2 * HD]
            values = packed_ref[:row_end, base + 2 * HD : base + 3 * HD]
            logits = score_block(seg_ref, query, keys, slope, row_start, tok_rows)
            top = jnp.max(logits, axis=0, keepdims=True)
            powers = jnp.exp(logits - top)
            total = jnp.sum(powers, axis=0, keepdims=True)
            probs = (powers * (1.0 / total)).astype(jnp.bfloat16)
            result = contract(values, probs, 0, 0)
            out_ref[rows, item * HD : (item + 1) * HD] = result.T.astype(jnp.bfloat16)
            total_ref[0, item : item + 1, rows] = top + jnp.log(total)


def backward_body(seg_ref, slope_ref, packed_ref, total_ref, grad_ref, out_ref, key_sum, value_sum):
    tok_rows = packed_ref.shape[0]
    group = pl.program_id(0)
    scale = HD ** (-0.5)
    for item in range(head_group):
        slope = slope_ref[group * head_group + item]
        base = item * 3 * HD
        for row_start in reversed(range(0, tok_rows, block_rows)):
            row_end = row_start + block_rows
            rows = slice(row_start, row_end)
            query = packed_ref[rows, base : base + HD] * jnp.bfloat16(scale)
            keys = packed_ref[:row_end, base + HD : base + 2 * HD]
            values = packed_ref[:row_end, base + 2 * HD : base + 3 * HD]
            grad = grad_ref[rows, item * HD : (item + 1) * HD]
            logits = score_block(seg_ref, query, keys, slope, row_start, tok_rows)
            probs = jnp.exp(logits - total_ref[0, item : item + 1, rows])
            grad_probs = contract(values, grad, 1, 1)
            weighted = jnp.sum(probs * grad_probs, axis=0, keepdims=True)
            grad_logits = (probs * (grad_probs - weighted)).astype(jnp.bfloat16)
            grad_query = contract(keys, grad_logits, 0, 0) * scale
            out_ref[rows, base : base + HD] = grad_query.T.astype(jnp.bfloat16)
            grad_key = contract(grad_logits, query, 1, 0)
            grad_value = contract(probs.astype(jnp.bfloat16), grad, 1, 0)
            if row_end == tok_rows:
                key_sum[...] = grad_key
                value_sum[...] = grad_value
            else:
                key_sum[:row_end, :] += grad_key
                value_sum[:row_end, :] += grad_value
        out_ref[:, base + HD : base + 2 * HD] = key_sum[...].astype(jnp.bfloat16)
        out_ref[:, base + 2 * HD : base + 3 * HD] = value_sum[...].astype(jnp.bfloat16)


def attend_specs(tok_rows):
    scalars = pl.BlockSpec(memory_space=pltpu.SMEM)
    packed = pl.BlockSpec((tok_rows, head_group * 3 * HD), lambda g: (0, g))
    totals = pl.BlockSpec((1, head_group, tok_rows), lambda g: (g, 0, 0))
    heads = pl.BlockSpec((tok_rows, head_group * HD), lambda g: (0, g))
    return scalars, packed, totals, heads


def attend_forward(packed, slopes, segments):
    tok_rows, width = packed.shape
    heads_here = width // (3 * HD)
    groups = heads_here // head_group
    scalars, packed_spec, totals, heads = attend_specs(tok_rows)
    return pl.pallas_call(
        forward_body,
        grid=(groups,),
        in_specs=[scalars, scalars, packed_spec],
        out_specs=[heads, totals],
        out_shape=[
            jax.ShapeDtypeStruct((tok_rows, heads_here * HD), jnp.bfloat16),
            jax.ShapeDtypeStruct((groups, head_group, tok_rows), jnp.float32),
        ],
        compiler_params=pltpu.CompilerParams(vmem_limit_bytes=40 * 2**20),
        cost_estimate=pl.CostEstimate(
            flops=4 * heads_here * tok_rows * tok_rows * HD,
            bytes_accessed=2 * tok_rows * width * 2,
            transcendentals=heads_here * tok_rows * tok_rows,
        ),
    )(segments, slopes, packed)


def attend_backward(packed, slopes, segments, log_totals, grad_attended):
    tok_rows, width = packed.shape
    heads_here = width // (3 * HD)
    scalars, packed_spec, totals, heads = attend_specs(tok_rows)
    return pl.pallas_call(
        backward_body,
        grid=(heads_here // head_group,),
        in_specs=[scalars, scalars, packed_spec, totals, heads],
        out_specs=packed_spec,
        out_shape=jax.ShapeDtypeStruct((tok_rows, width), jnp.bfloat16),
        scratch_shapes=[
            pltpu.VMEM((tok_rows, HD), jnp.float32),
            pltpu.VMEM((tok_rows, HD), jnp.float32),
        ],
        compiler_params=pltpu.CompilerParams(vmem_limit_bytes=40 * 2**20),
        cost_estimate=pl.CostEstimate(
            flops=10 * heads_here * tok_rows * tok_rows * HD,
            bytes_accessed=3 * tok_rows * width * 2,
            transcendentals=heads_here * tok_rows * tok_rows,
        ),
    )(segments, slopes, packed, log_totals, grad_attended)


def exchange_body(scatter, axis, devices, *refs):
    count = len(scatter)
    sources, results = refs[:count], refs[count : 2 * count]
    local_sem, send_sem, recv_sem = refs[2 * count :]
    me = lax.axis_index(axis)

    barrier = pltpu.get_barrier_semaphore()

    def greet(step, carry):
        peer = lax.rem(me + step, devices)
        pl.semaphore_signal(
            barrier, inc=1, device_id={axis: peer}, device_id_type=pl.DeviceIdType.MESH
        )
        return carry

    lax.fori_loop(1, devices, greet, 0)
    pl.semaphore_wait(barrier, devices - 1)

    def block_of(item, owner):
        return sources[item].at[owner] if scatter[item] else sources[item]

    def copy_to(item, step):
        peer = lax.rem(me + step, devices)
        return pltpu.make_async_remote_copy(
            src_ref=block_of(item, peer),
            dst_ref=results[item].at[me],
            send_sem=send_sem.at[item, step],
            recv_sem=recv_sem.at[item, step],
            device_id={axis: peer},
            device_id_type=pl.DeviceIdType.MESH,
        )

    def own_copy(item):
        return pltpu.make_async_copy(
            block_of(item, me), results[item].at[me], local_sem.at[item]
        )

    def start(step, carry):
        for item in range(count):
            copy_to(item, step).start()
        return carry

    def finish(step, carry):
        for item in range(count):
            copy_to(item, step).wait()
        return carry

    lax.fori_loop(1, devices, start, 0)
    for item in range(count):
        own_copy(item).start()
    for item in range(count):
        own_copy(item).wait()
    lax.fori_loop(1, devices, finish, 0)


def exchange(sources, scatter, axis, call_id):
    devices = lax.axis_size(axis)
    count = len(sources)
    shapes = [item.shape[1:] if apart else item.shape for apart, item in zip(scatter, sources)]
    size = sum(devices * rows * width * 2 for rows, width in shapes)
    return pl.pallas_call(
        partial(exchange_body, scatter, axis, devices),
        in_specs=[pl.BlockSpec(memory_space=pl.ANY)] * count,
        out_specs=[pl.BlockSpec(memory_space=pl.ANY)] * count,
        out_shape=[
            jax.ShapeDtypeStruct((devices, *shape), item.dtype)
            for shape, item in zip(shapes, sources)
        ],
        scratch_shapes=[
            pltpu.SemaphoreType.DMA((count,)),
            pltpu.SemaphoreType.DMA((count, devices)),
            pltpu.SemaphoreType.DMA((count, devices)),
        ],
        compiler_params=pltpu.CompilerParams(collective_id=call_id, has_side_effects=True),
        cost_estimate=pl.CostEstimate(flops=0, bytes_accessed=20 * size, transcendentals=0),
    )(*sources)


def gather_rows(sources, call_id):
    gathered = exchange(sources, (False,) * len(sources), "wide", call_id)
    return [item.reshape(-1, item.shape[-1]) for item in gathered]


def scatter_sums(sources, call_id, whole=()):
    devices = lax.axis_size("wide")
    blocks = [item.reshape(devices, -1, item.shape[-1]) for item in sources]
    scatter = (True,) * len(blocks) + (False,) * len(whole)
    parts = exchange([*blocks, *whole], scatter, "wide", call_id)
    return [jnp.sum(item.astype(jnp.float32), axis=0) for item in parts]


def local(
    tokens,
    segments,
    first_gain,
    first_shift,
    qkv_weight,
    qv_bias,
    dense_weight,
    dense_bias,
    second_gain,
    second_shift,
    up_weight,
    up_bias,
    down_weight,
    down_bias,
    cotangent,
):
    tok_rows, local_width = tokens.shape
    col_start = lax.axis_index("narrow") * local_width
    heads_here = qv_bias.shape[0] // (2 * HD)
    head_first = lax.axis_index("narrow") * heads_here
    slopes = 2.0 ** (-8.0 * (head_first + jnp.arange(heads_here) + 1).astype(jnp.float32) / H)
    out_rows = dense_weight.shape[1]
    vectors = jnp.stack([first_gain, first_shift, dense_bias, second_gain, second_shift])
    vectors = jnp.pad(vectors, ((0, 11), (0, 0)))
    joined = lax.all_gather(
        jnp.concatenate([tokens, dense_weight.T, vectors], axis=0), "narrow", axis=1, tiled=True
    )
    full_tokens = joined[:tok_rows]
    dense_block = joined[tok_rows : tok_rows + out_rows]
    gain_one, shift_one, bias_dense, gain_two, shift_two = (
        joined[tok_rows + out_rows + item].astype(jnp.float32) for item in range(5)
    )
    qkv_full, up_full = gather_rows([qkv_weight, up_weight], 0)
    grad_out = lax.all_gather(cotangent, "narrow", axis=1, tiled=True)
    inputs = full_tokens.astype(jnp.float32)
    normed_one, hat_one, inv_one = normalize(inputs, gain_one, shift_one)
    act_one = normed_one.astype(jnp.bfloat16)
    bias_pair = qv_bias.astype(jnp.float32).reshape(heads_here, 2, HD)
    full_bias = jnp.stack(
        [bias_pair[:, 0], jnp.zeros_like(bias_pair[:, 0]), bias_pair[:, 1]], axis=1
    ).reshape(-1)
    packed = (
        jnp.dot(act_one, qkv_full, preferred_element_type=jnp.float32) + full_bias[None]
    ).astype(jnp.bfloat16)
    attended, log_totals = attend_forward(packed, slopes, segments)
    attended_full = lax.all_gather(attended, "narrow", axis=1, tiled=True)
    dense_rows, down_rows = gather_rows([dense_block, down_weight.T], 1)
    mixed = contract(attended_full, dense_rows, 1, 1)
    residual = inputs + (mixed + bias_dense)
    normed_two, hat_two, inv_two = normalize(residual, gain_two, shift_two)
    act_two = normed_two.astype(jnp.bfloat16)
    pre_act = jnp.dot(act_two, up_full, preferred_element_type=jnp.float32) + up_bias.astype(
        jnp.float32
    )
    hidden = jax.nn.gelu(pre_act, approximate=True).astype(jnp.bfloat16)
    grad_hidden = jnp.dot(grad_out, down_rows, preferred_element_type=jnp.float32)
    _, gelu_back = jax.vjp(partial(jax.nn.gelu, approximate=True), pre_act)
    grad_pre = gelu_back(grad_hidden)[0].astype(jnp.bfloat16)
    grad_act_two = lax.psum(
        contract(grad_pre, up_full, 1, 1).astype(jnp.bfloat16), "narrow"
    )
    mlp_out = lax.psum_scatter(
        contract(hidden, down_rows, 1, 1).astype(jnp.bfloat16),
        "narrow",
        scatter_dimension=1,
        tiled=True,
    ).astype(jnp.float32)
    output = (
        own_columns(residual, col_start, local_width) + (mlp_out + down_bias.astype(jnp.float32))
    ).astype(jnp.bfloat16)
    down_bias_grad = jnp.sum(cotangent.astype(jnp.float32), axis=0)
    up_bias_grad = jnp.sum(grad_pre.astype(jnp.float32), axis=0)
    grad_down = contract(grad_out, hidden, 0, 0).astype(jnp.bfloat16)
    grad_up = contract(act_two, grad_pre, 0, 0).astype(jnp.bfloat16)
    up_weight_grad, down_rows_grad = scatter_sums([grad_up, grad_down], 2)
    grad_act_two, up_weight_grad, down_rows_grad = lax.optimization_barrier(
        (grad_act_two, up_weight_grad, down_rows_grad)
    )
    grad_act_two = grad_act_two.astype(jnp.float32)
    second_gain_grad = own_columns(jnp.sum(grad_act_two * hat_two, axis=0), col_start, local_width)
    second_shift_grad = own_columns(jnp.sum(grad_act_two, axis=0), col_start, local_width)
    grad_residual = grad_out.astype(jnp.float32) + norm_backward(
        grad_act_two, gain_two, hat_two, inv_two
    )
    grad_branch = grad_residual.astype(jnp.bfloat16)
    dense_bias_grad = own_columns(
        jnp.sum(grad_branch.astype(jnp.float32), axis=0), col_start, local_width
    )
    grad_attended = jnp.dot(
        grad_branch,
        own_columns(dense_rows, col_start, local_width),
        preferred_element_type=jnp.float32,
    ).astype(jnp.bfloat16)
    grad_packed = attend_backward(packed, slopes, segments, log_totals, grad_attended)
    column_sums = jnp.sum(grad_packed.astype(jnp.float32), axis=0).reshape(heads_here, 3, HD)
    qv_bias_grad = jnp.stack([column_sums[:, 0], column_sums[:, 2]], axis=1).reshape(-1)
    grad_one_part = contract(grad_packed, qkv_full, 1, 1)
    grad_act_one = lax.psum_scatter(
        grad_one_part.astype(jnp.bfloat16), "narrow", scatter_dimension=1, tiled=True
    ).astype(jnp.float32)
    scaled_part = grad_one_part * gain_one
    row_sums = jnp.stack([jnp.sum(scaled_part, axis=1), jnp.sum(scaled_part * hat_one, axis=1)])
    feature_sums = jnp.stack(
        [jnp.sum(grad_one_part * hat_one, axis=0), jnp.sum(grad_one_part, axis=0)]
    )
    lines = jnp.concatenate([row_sums.reshape(-1, 128), feature_sums.reshape(-1, 128)], axis=0)
    (line_parts,) = exchange([lines], (False,), "narrow", 4)
    flat_sums = jnp.sum(line_parts, axis=0).reshape(-1)
    sum_plain, sum_hat = flat_sums[: 2 * tok_rows].reshape(2, tok_rows)
    gain_part, shift_part = flat_sums[2 * tok_rows :].reshape(2, -1)
    grad_qkv = contract(act_one, grad_packed, 0, 0).astype(jnp.bfloat16)
    grad_dense = contract(grad_branch, attended, 0, 0).astype(jnp.bfloat16)
    small = (
        own_columns(gain_part, col_start, local_width),
        own_columns(shift_part, col_start, local_width),
        qv_bias_grad,
        dense_bias_grad,
        second_gain_grad,
        second_shift_grad,
        up_bias_grad,
        down_bias_grad,
    )
    qkv_weight_grad, dense_rows_grad, small_sums = scatter_sums(
        [grad_qkv, grad_dense], 3, [jnp.concatenate(small).reshape(-1, 128)]
    )
    small_sums = small_sums.reshape(-1)
    bounds = [0]
    for item in small:
        bounds.append(bounds[-1] + item.shape[0])
    (
        first_gain_grad,
        first_shift_grad,
        qv_bias_grad,
        dense_bias_grad,
        second_gain_grad,
        second_shift_grad,
        up_bias_grad,
        down_bias_grad,
    ) = (small_sums[low:high] for low, high in zip(bounds, bounds[1:]))
    hat_local = own_columns(hat_one, col_start, local_width)
    scaled = grad_act_one * first_gain.astype(jnp.float32)
    full_width = local_width * lax.axis_size("narrow")
    grad_norm_one = inv_one * (
        scaled - sum_plain[:, None] / full_width - hat_local * sum_hat[:, None] / full_width
    )
    token_grad = (own_columns(grad_residual, col_start, local_width) + grad_norm_one).astype(
        jnp.bfloat16
    )
    dense_weight_grad = dense_rows_grad.T
    down_weight_grad = down_rows_grad.T
    return (
        output,
        token_grad,
        first_gain_grad,
        first_shift_grad,
        qkv_weight_grad,
        qv_bias_grad,
        dense_weight_grad,
        dense_bias_grad,
        second_gain_grad,
        second_shift_grad,
        up_weight_grad,
        up_bias_grad,
        down_weight_grad,
        down_bias_grad,
    )


def solution(mesh):
    in_specs = (
        P("wide", "narrow"),
        P("wide"),
        P("narrow"),
        P("narrow"),
        P("wide", "narrow"),
        P("narrow"),
        P("narrow", "wide"),
        P("narrow"),
        P("narrow"),
        P("narrow"),
        P("wide", "narrow"),
        P("narrow"),
        P("narrow", "wide"),
        P("narrow"),
        P("wide", "narrow"),
    )
    out_specs = (
        P("wide", "narrow"),
        P("wide", "narrow"),
        P("narrow"),
        P("narrow"),
        P("wide", "narrow"),
        P("narrow"),
        P("narrow", "wide"),
        P("narrow"),
        P("narrow"),
        P("narrow"),
        P("wide", "narrow"),
        P("narrow"),
        P("narrow", "wide"),
        P("narrow"),
    )
    return jax.shard_map(local, mesh=mesh, in_specs=in_specs, out_specs=out_specs, check_vma=False)
```

```python
from functools import partial

import jax
import jax.numpy as jnp
from jax import lax
from jax.experimental import pallas as pl
from jax.experimental.pallas import tpu as pltpu
from jax.sharding import PartitionSpec as P

H = 16
HD = 64


eps = 1e-05
negative = -1e30
block_rows = 256
head_group = 2


def normalize(values, gain, shift):
    mean_value = jnp.mean(values, axis=-1, keepdims=True)
    centered = values - mean_value
    inv_std = lax.rsqrt(jnp.mean(centered * centered, axis=-1, keepdims=True) + eps)
    normed = centered * inv_std
    return (normed * gain + shift, normed, inv_std)


def norm_backward(grad_norm, gain, normed, inv_std):
    scaled = grad_norm * gain
    mean_one = jnp.mean(scaled, axis=-1, keepdims=True)
    mean_two = jnp.mean(scaled * normed, axis=-1, keepdims=True)
    return inv_std * (scaled - mean_one - normed * mean_two)


def own_columns(values, col_start, local_width):
    return lax.dynamic_slice_in_dim(values, col_start, local_width, values.ndim - 1)


def contract(left, right, left_dim, right_dim):
    return lax.dot_general(
        left, right, (((left_dim,), (right_dim,)), ((), ())), preferred_element_type=jnp.float32
    )


def score_block(seg_ref, query_block, keys, slope, row_start, tok_rows):
    row_end = keys.shape[0]
    logits = contract(keys, query_block, 1, 1)
    key_pos = lax.broadcasted_iota(jnp.int32, (row_end, 1), 0)
    query_pos = row_start + lax.broadcasted_iota(jnp.int32, (1, query_block.shape[0]), 1)
    half = tok_rows // 2
    shared = (seg_ref[0] == seg_ref[half]).astype(jnp.int32)
    first_key = 0 if row_start < half else jnp.where(shared == 1, 0, half)
    key_term = slope * (key_pos - row_start).astype(jnp.float32)
    allowed = (key_pos <= query_pos) & (key_pos >= first_key)
    return jnp.where(allowed, logits + key_term, negative)


def forward_body(seg_ref, slope_ref, packed_ref, out_ref, total_ref):
    tok_rows = packed_ref.shape[0]
    group = pl.program_id(0)
    for item in range(head_group):
        slope = slope_ref[group * head_group + item]
        base = item * 3 * HD
        for row_start in range(0, tok_rows, block_rows):
            row_end = row_start + block_rows
            rows = slice(row_start, row_end)
            query = packed_ref[rows, base : base + HD] * jnp.bfloat16(HD ** (-0.5))
            keys = packed_ref[:row_end, base + HD : base + 2 * HD]
            values = packed_ref[:row_end, base + 2 * HD : base + 3 * HD]
            logits = score_block(seg_ref, query, keys, slope, row_start, tok_rows)
            top = jnp.max(logits, axis=0, keepdims=True)
            powers = jnp.exp(logits - top)
            total = jnp.sum(powers, axis=0, keepdims=True)
            probs = (powers * (1.0 / total)).astype(jnp.bfloat16)
            result = contract(values, probs, 0, 0)
            out_ref[rows, item * HD : (item + 1) * HD] = result.T.astype(jnp.bfloat16)
            total_ref[0, item : item + 1, rows] = top + jnp.log(total)


def backward_body(seg_ref, slope_ref, packed_ref, total_ref, grad_ref, out_ref, key_sum, value_sum):
    tok_rows = packed_ref.shape[0]
    group = pl.program_id(0)
    scale = HD ** (-0.5)
    for item in range(head_group):
        slope = slope_ref[group * head_group + item]
        base = item * 3 * HD
        for row_start in reversed(range(0, tok_rows, block_rows)):
            row_end = row_start + block_rows
            rows = slice(row_start, row_end)
            query = packed_ref[rows, base : base + HD] * jnp.bfloat16(scale)
            keys = packed_ref[:row_end, base + HD : base + 2 * HD]
            values = packed_ref[:row_end, base + 2 * HD : base + 3 * HD]
            grad = grad_ref[rows, item * HD : (item + 1) * HD]
            logits = score_block(seg_ref, query, keys, slope, row_start, tok_rows)
            probs = jnp.exp(logits - total_ref[0, item : item + 1, rows])
            grad_probs = contract(values, grad, 1, 1)
            weighted = jnp.sum(probs * grad_probs, axis=0, keepdims=True)
            grad_logits = (probs * (grad_probs - weighted)).astype(jnp.bfloat16)
            grad_query = contract(keys, grad_logits, 0, 0) * scale
            out_ref[rows, base : base + HD] = grad_query.T.astype(jnp.bfloat16)
            grad_key = contract(grad_logits, query, 1, 0)
            grad_value = contract(probs.astype(jnp.bfloat16), grad, 1, 0)
            if row_end == tok_rows:
                key_sum[...] = grad_key
                value_sum[...] = grad_value
            else:
                key_sum[:row_end, :] += grad_key
                value_sum[:row_end, :] += grad_value
        out_ref[:, base + HD : base + 2 * HD] = key_sum[...].astype(jnp.bfloat16)
        out_ref[:, base + 2 * HD : base + 3 * HD] = value_sum[...].astype(jnp.bfloat16)


def attend_specs(tok_rows):
    scalars = pl.BlockSpec(memory_space=pltpu.SMEM)
    packed = pl.BlockSpec((tok_rows, head_group * 3 * HD), lambda g: (0, g))
    totals = pl.BlockSpec((1, head_group, tok_rows), lambda g: (g, 0, 0))
    heads = pl.BlockSpec((tok_rows, head_group * HD), lambda g: (0, g))
    return scalars, packed, totals, heads


def attend_forward(packed, slopes, segments):
    tok_rows, width = packed.shape
    heads_here = width // (3 * HD)
    groups = heads_here // head_group
    scalars, packed_spec, totals, heads = attend_specs(tok_rows)
    return pl.pallas_call(
        forward_body,
        grid=(groups,),
        in_specs=[scalars, scalars, packed_spec],
        out_specs=[heads, totals],
        out_shape=[
            jax.ShapeDtypeStruct((tok_rows, heads_here * HD), jnp.bfloat16),
            jax.ShapeDtypeStruct((groups, head_group, tok_rows), jnp.float32),
        ],
        compiler_params=pltpu.CompilerParams(vmem_limit_bytes=40 * 2**20),
        cost_estimate=pl.CostEstimate(
            flops=4 * heads_here * tok_rows * tok_rows * HD,
            bytes_accessed=2 * tok_rows * width * 2,
            transcendentals=heads_here * tok_rows * tok_rows,
        ),
    )(segments, slopes, packed)


def attend_backward(packed, slopes, segments, log_totals, grad_attended):
    tok_rows, width = packed.shape
    heads_here = width // (3 * HD)
    scalars, packed_spec, totals, heads = attend_specs(tok_rows)
    return pl.pallas_call(
        backward_body,
        grid=(heads_here // head_group,),
        in_specs=[scalars, scalars, packed_spec, totals, heads],
        out_specs=packed_spec,
        out_shape=jax.ShapeDtypeStruct((tok_rows, width), jnp.bfloat16),
        scratch_shapes=[
            pltpu.VMEM((tok_rows, HD), jnp.float32),
            pltpu.VMEM((tok_rows, HD), jnp.float32),
        ],
        compiler_params=pltpu.CompilerParams(vmem_limit_bytes=40 * 2**20),
        cost_estimate=pl.CostEstimate(
            flops=10 * heads_here * tok_rows * tok_rows * HD,
            bytes_accessed=3 * tok_rows * width * 2,
            transcendentals=heads_here * tok_rows * tok_rows,
        ),
    )(segments, slopes, packed, log_totals, grad_attended)


def exchange_body(scatter, axis, devices, *refs):
    count = len(scatter)
    sources, results = refs[:count], refs[count : 2 * count]
    local_sem, send_sem, recv_sem = refs[2 * count :]
    me = lax.axis_index(axis)

    barrier = pltpu.get_barrier_semaphore()

    def greet(step, carry):
        peer = lax.rem(me + step, devices)
        pl.semaphore_signal(
            barrier, inc=1, device_id={axis: peer}, device_id_type=pl.DeviceIdType.MESH
        )
        return carry

    lax.fori_loop(1, devices, greet, 0)
    pl.semaphore_wait(barrier, devices - 1)

    def block_of(item, owner):
        return sources[item].at[owner] if scatter[item] else sources[item]

    def copy_to(item, step):
        peer = lax.rem(me + step, devices)
        return pltpu.make_async_remote_copy(
            src_ref=block_of(item, peer),
            dst_ref=results[item].at[me],
            send_sem=send_sem.at[item, step],
            recv_sem=recv_sem.at[item, step],
            device_id={axis: peer},
            device_id_type=pl.DeviceIdType.MESH,
        )

    def own_copy(item):
        return pltpu.make_async_copy(
            block_of(item, me), results[item].at[me], local_sem.at[item]
        )

    def start(step, carry):
        for item in range(count):
            copy_to(item, step).start()
        return carry

    def finish(step, carry):
        for item in range(count):
            copy_to(item, step).wait()
        return carry

    lax.fori_loop(1, devices, start, 0)
    for item in range(count):
        own_copy(item).start()
    for item in range(count):
        own_copy(item).wait()
    lax.fori_loop(1, devices, finish, 0)


def exchange(sources, scatter, axis, call_id):
    devices = lax.axis_size(axis)
    count = len(sources)
    shapes = [item.shape[1:] if apart else item.shape for apart, item in zip(scatter, sources)]
    size = sum(devices * rows * width * 2 for rows, width in shapes)
    return pl.pallas_call(
        partial(exchange_body, scatter, axis, devices),
        in_specs=[pl.BlockSpec(memory_space=pl.ANY)] * count,
        out_specs=[pl.BlockSpec(memory_space=pl.ANY)] * count,
        out_shape=[
            jax.ShapeDtypeStruct((devices, *shape), item.dtype)
            for shape, item in zip(shapes, sources)
        ],
        scratch_shapes=[
            pltpu.SemaphoreType.DMA((count,)),
            pltpu.SemaphoreType.DMA((count, devices)),
            pltpu.SemaphoreType.DMA((count, devices)),
        ],
        compiler_params=pltpu.CompilerParams(collective_id=call_id, has_side_effects=True),
        cost_estimate=pl.CostEstimate(flops=0, bytes_accessed=20 * size, transcendentals=0),
    )(*sources)


def gather_rows(sources, call_id):
    gathered = exchange(sources, (False,) * len(sources), "wide", call_id)
    return [item.reshape(-1, item.shape[-1]) for item in gathered]


def scatter_sums(sources, call_id, whole=()):
    devices = lax.axis_size("wide")
    blocks = [item.reshape(devices, -1, item.shape[-1]) for item in sources]
    scatter = (True,) * len(blocks) + (False,) * len(whole)
    parts = exchange([*blocks, *whole], scatter, "wide", call_id)
    return [jnp.sum(item.astype(jnp.float32), axis=0) for item in parts]


def local(
    tokens,
    segments,
    first_gain,
    first_shift,
    qkv_weight,
    qv_bias,
    dense_weight,
    dense_bias,
    second_gain,
    second_shift,
    up_weight,
    up_bias,
    down_weight,
    down_bias,
    cotangent,
):
    tok_rows, local_width = tokens.shape
    col_start = lax.axis_index("narrow") * local_width
    heads_here = qv_bias.shape[0] // (2 * HD)
    head_first = lax.axis_index("narrow") * heads_here
    slopes = 2.0 ** (-8.0 * (head_first + jnp.arange(heads_here) + 1).astype(jnp.float32) / H)
    out_rows = dense_weight.shape[1]
    vectors = jnp.stack([first_gain, first_shift, dense_bias, second_gain, second_shift])
    vectors = jnp.pad(vectors, ((0, 11), (0, 0)))
    joined = lax.all_gather(
        jnp.concatenate([tokens, dense_weight.T, vectors], axis=0), "narrow", axis=1, tiled=True
    )
    full_tokens = joined[:tok_rows]
    dense_block = joined[tok_rows : tok_rows + out_rows]
    gain_one, shift_one, bias_dense, gain_two, shift_two = (
        joined[tok_rows + out_rows + item].astype(jnp.float32) for item in range(5)
    )
    qkv_full, up_full = gather_rows([qkv_weight, up_weight], 0)
    grad_out = lax.all_gather(cotangent, "narrow", axis=1, tiled=True)
    inputs = full_tokens.astype(jnp.float32)
    normed_one, hat_one, inv_one = normalize(inputs, gain_one, shift_one)
    act_one = normed_one.astype(jnp.bfloat16)
    bias_pair = qv_bias.astype(jnp.float32).reshape(heads_here, 2, HD)
    full_bias = jnp.stack(
        [bias_pair[:, 0], jnp.zeros_like(bias_pair[:, 0]), bias_pair[:, 1]], axis=1
    ).reshape(-1)
    packed = (
        jnp.dot(act_one, qkv_full, preferred_element_type=jnp.float32) + full_bias[None]
    ).astype(jnp.bfloat16)
    attended, log_totals = attend_forward(packed, slopes, segments)
    attended_full = lax.all_gather(attended, "narrow", axis=1, tiled=True)
    dense_block, grad_out = lax.optimization_barrier((dense_block, grad_out))
    dense_rows, down_rows = gather_rows([dense_block, down_weight.T], 1)
    mixed = contract(attended_full, dense_rows, 1, 1)
    residual = inputs + (mixed + bias_dense)
    normed_two, hat_two, inv_two = normalize(residual, gain_two, shift_two)
    act_two = normed_two.astype(jnp.bfloat16)
    pre_act = jnp.dot(act_two, up_full, preferred_element_type=jnp.float32) + up_bias.astype(
        jnp.float32
    )
    hidden = jax.nn.gelu(pre_act, approximate=True).astype(jnp.bfloat16)
    grad_hidden = jnp.dot(grad_out, down_rows, preferred_element_type=jnp.float32)
    _, gelu_back = jax.vjp(partial(jax.nn.gelu, approximate=True), pre_act)
    grad_pre = gelu_back(grad_hidden)[0].astype(jnp.bfloat16)
    grad_act_two = lax.psum(
        contract(grad_pre, up_full, 1, 1).astype(jnp.bfloat16), "narrow"
    )
    mlp_out = lax.psum_scatter(
        contract(hidden, down_rows, 1, 1).astype(jnp.bfloat16),
        "narrow",
        scatter_dimension=1,
        tiled=True,
    ).astype(jnp.float32)
    output = (
        own_columns(residual, col_start, local_width) + (mlp_out + down_bias.astype(jnp.float32))
    ).astype(jnp.bfloat16)
    down_bias_grad = jnp.sum(cotangent.astype(jnp.float32), axis=0)
    up_bias_grad = jnp.sum(grad_pre.astype(jnp.float32), axis=0)
    grad_down = contract(grad_out, hidden, 0, 0).astype(jnp.bfloat16)
    grad_up = contract(act_two, grad_pre, 0, 0).astype(jnp.bfloat16)
    up_weight_grad, down_rows_grad = scatter_sums([grad_up, grad_down], 2)
    grad_act_two, up_weight_grad, down_rows_grad = lax.optimization_barrier(
        (grad_act_two, up_weight_grad, down_rows_grad)
    )
    grad_act_two = grad_act_two.astype(jnp.float32)
    second_gain_grad = own_columns(jnp.sum(grad_act_two * hat_two, axis=0), col_start, local_width)
    second_shift_grad = own_columns(jnp.sum(grad_act_two, axis=0), col_start, local_width)
    grad_residual = grad_out.astype(jnp.float32) + norm_backward(
        grad_act_two, gain_two, hat_two, inv_two
    )
    grad_branch = grad_residual.astype(jnp.bfloat16)
    dense_bias_grad = own_columns(
        jnp.sum(grad_branch.astype(jnp.float32), axis=0), col_start, local_width
    )
    grad_attended = jnp.dot(
        grad_branch,
        own_columns(dense_rows, col_start, local_width),
        preferred_element_type=jnp.float32,
    ).astype(jnp.bfloat16)
    grad_packed = attend_backward(packed, slopes, segments, log_totals, grad_attended)
    column_sums = jnp.sum(grad_packed.astype(jnp.float32), axis=0).reshape(heads_here, 3, HD)
    qv_bias_grad = jnp.stack([column_sums[:, 0], column_sums[:, 2]], axis=1).reshape(-1)
    grad_one_part = contract(grad_packed, qkv_full, 1, 1)
    grad_act_one = lax.psum_scatter(
        grad_one_part.astype(jnp.bfloat16), "narrow", scatter_dimension=1, tiled=True
    ).astype(jnp.float32)
    scaled_part = grad_one_part * gain_one
    row_sums = jnp.stack([jnp.sum(scaled_part, axis=1), jnp.sum(scaled_part * hat_one, axis=1)])
    feature_sums = jnp.stack(
        [jnp.sum(grad_one_part * hat_one, axis=0), jnp.sum(grad_one_part, axis=0)]
    )
    lines = jnp.concatenate([row_sums.reshape(-1, 128), feature_sums.reshape(-1, 128)], axis=0)
    (line_parts,) = exchange([lines], (False,), "narrow", 4)
    flat_sums = jnp.sum(line_parts, axis=0).reshape(-1)
    sum_plain, sum_hat = flat_sums[: 2 * tok_rows].reshape(2, tok_rows)
    gain_part, shift_part = flat_sums[2 * tok_rows :].reshape(2, -1)
    grad_qkv = contract(act_one, grad_packed, 0, 0).astype(jnp.bfloat16)
    grad_dense = contract(grad_branch, attended, 0, 0).astype(jnp.bfloat16)
    small = (
        own_columns(gain_part, col_start, local_width),
        own_columns(shift_part, col_start, local_width),
        qv_bias_grad,
        dense_bias_grad,
        second_gain_grad,
        second_shift_grad,
        up_bias_grad,
        down_bias_grad,
    )
    qkv_weight_grad, dense_rows_grad, small_sums = scatter_sums(
        [grad_qkv, grad_dense], 3, [jnp.concatenate(small).reshape(-1, 128)]
    )
    small_sums = small_sums.reshape(-1)
    bounds = [0]
    for item in small:
        bounds.append(bounds[-1] + item.shape[0])
    (
        first_gain_grad,
        first_shift_grad,
        qv_bias_grad,
        dense_bias_grad,
        second_gain_grad,
        second_shift_grad,
        up_bias_grad,
        down_bias_grad,
    ) = (small_sums[low:high] for low, high in zip(bounds, bounds[1:]))
    hat_local = own_columns(hat_one, col_start, local_width)
    scaled = grad_act_one * first_gain.astype(jnp.float32)
    full_width = local_width * lax.axis_size("narrow")
    grad_norm_one = inv_one * (
        scaled - sum_plain[:, None] / full_width - hat_local * sum_hat[:, None] / full_width
    )
    token_grad = (own_columns(grad_residual, col_start, local_width) + grad_norm_one).astype(
        jnp.bfloat16
    )
    dense_weight_grad = dense_rows_grad.T
    down_weight_grad = down_rows_grad.T
    return (
        output,
        token_grad,
        first_gain_grad,
        first_shift_grad,
        qkv_weight_grad,
        qv_bias_grad,
        dense_weight_grad,
        dense_bias_grad,
        second_gain_grad,
        second_shift_grad,
        up_weight_grad,
        up_bias_grad,
        down_weight_grad,
        down_bias_grad,
    )


def solution(mesh):
    in_specs = (
        P("wide", "narrow"),
        P("wide"),
        P("narrow"),
        P("narrow"),
        P("wide", "narrow"),
        P("narrow"),
        P("narrow", "wide"),
        P("narrow"),
        P("narrow"),
        P("narrow"),
        P("wide", "narrow"),
        P("narrow"),
        P("narrow", "wide"),
        P("narrow"),
        P("wide", "narrow"),
    )
    out_specs = (
        P("wide", "narrow"),
        P("wide", "narrow"),
        P("narrow"),
        P("narrow"),
        P("wide", "narrow"),
        P("narrow"),
        P("narrow", "wide"),
        P("narrow"),
        P("narrow"),
        P("narrow"),
        P("wide", "narrow"),
        P("narrow"),
        P("narrow", "wide"),
        P("narrow"),
    )
    return jax.shard_map(local, mesh=mesh, in_specs=in_specs, out_specs=out_specs, check_vma=False)
```

```python
from functools import partial

import jax
import jax.numpy as jnp
from jax import lax
from jax.experimental import pallas as pl
from jax.experimental.pallas import tpu as pltpu
from jax.sharding import PartitionSpec as P

H = 16
HD = 64


eps = 1e-05
negative = -1e30
block_rows = 256
head_group = 2


def normalize(values, gain, shift):
    mean_value = jnp.mean(values, axis=-1, keepdims=True)
    centered = values - mean_value
    inv_std = lax.rsqrt(jnp.mean(centered * centered, axis=-1, keepdims=True) + eps)
    normed = centered * inv_std
    return (normed * gain + shift, normed, inv_std)


def norm_backward(grad_norm, gain, normed, inv_std):
    scaled = grad_norm * gain
    mean_one = jnp.mean(scaled, axis=-1, keepdims=True)
    mean_two = jnp.mean(scaled * normed, axis=-1, keepdims=True)
    return inv_std * (scaled - mean_one - normed * mean_two)


def own_columns(values, col_start, local_width):
    return lax.dynamic_slice_in_dim(values, col_start, local_width, values.ndim - 1)


def contract(left, right, left_dim, right_dim):
    return lax.dot_general(
        left, right, (((left_dim,), (right_dim,)), ((), ())), preferred_element_type=jnp.float32
    )


def score_block(seg_ref, query_block, keys, slope, row_start, tok_rows):
    row_end = keys.shape[0]
    logits = contract(keys, query_block, 1, 1)
    key_pos = lax.broadcasted_iota(jnp.int32, (row_end, 1), 0)
    query_pos = row_start + lax.broadcasted_iota(jnp.int32, (1, query_block.shape[0]), 1)
    half = tok_rows // 2
    shared = (seg_ref[0] == seg_ref[half]).astype(jnp.int32)
    first_key = 0 if row_start < half else jnp.where(shared == 1, 0, half)
    key_term = slope * (key_pos - row_start).astype(jnp.float32)
    allowed = (key_pos <= query_pos) & (key_pos >= first_key)
    return jnp.where(allowed, logits + key_term, negative)


def forward_body(seg_ref, slope_ref, packed_ref, out_ref, total_ref):
    tok_rows = packed_ref.shape[0]
    group = pl.program_id(0)
    for item in range(head_group):
        slope = slope_ref[group * head_group + item]
        base = item * 3 * HD
        for row_start in range(0, tok_rows, block_rows):
            row_end = row_start + block_rows
            rows = slice(row_start, row_end)
            query = packed_ref[rows, base : base + HD] * jnp.bfloat16(HD ** (-0.5))
            keys = packed_ref[:row_end, base + HD : base + 2 * HD]
            values = packed_ref[:row_end, base + 2 * HD : base + 3 * HD]
            logits = score_block(seg_ref, query, keys, slope, row_start, tok_rows)
            top = jnp.max(logits, axis=0, keepdims=True)
            powers = jnp.exp(logits - top)
            total = jnp.sum(powers, axis=0, keepdims=True)
            probs = (powers * (1.0 / total)).astype(jnp.bfloat16)
            result = contract(values, probs, 0, 0)
            out_ref[rows, item * HD : (item + 1) * HD] = result.T.astype(jnp.bfloat16)
            total_ref[0, item : item + 1, rows] = top + jnp.log(total)


def backward_body(seg_ref, slope_ref, packed_ref, total_ref, grad_ref, out_ref, key_sum, value_sum):
    tok_rows = packed_ref.shape[0]
    group = pl.program_id(0)
    scale = HD ** (-0.5)
    for item in range(head_group):
        slope = slope_ref[group * head_group + item]
        base = item * 3 * HD
        for row_start in reversed(range(0, tok_rows, block_rows)):
            row_end = row_start + block_rows
            rows = slice(row_start, row_end)
            query = packed_ref[rows, base : base + HD] * jnp.bfloat16(scale)
            keys = packed_ref[:row_end, base + HD : base + 2 * HD]
            values = packed_ref[:row_end, base + 2 * HD : base + 3 * HD]
            grad = grad_ref[rows, item * HD : (item + 1) * HD]
            logits = score_block(seg_ref, query, keys, slope, row_start, tok_rows)
            probs = jnp.exp(logits - total_ref[0, item : item + 1, rows])
            grad_probs = contract(values, grad, 1, 1)
            weighted = jnp.sum(probs * grad_probs, axis=0, keepdims=True)
            grad_logits = (probs * (grad_probs - weighted)).astype(jnp.bfloat16)
            grad_query = contract(keys, grad_logits, 0, 0) * scale
            out_ref[rows, base : base + HD] = grad_query.T.astype(jnp.bfloat16)
            grad_key = contract(grad_logits, query, 1, 0)
            grad_value = contract(probs.astype(jnp.bfloat16), grad, 1, 0)
            if row_end == tok_rows:
                key_sum[...] = grad_key
                value_sum[...] = grad_value
            else:
                key_sum[:row_end, :] += grad_key
                value_sum[:row_end, :] += grad_value
        out_ref[:, base + HD : base + 2 * HD] = key_sum[...].astype(jnp.bfloat16)
        out_ref[:, base + 2 * HD : base + 3 * HD] = value_sum[...].astype(jnp.bfloat16)


def attend_specs(tok_rows):
    scalars = pl.BlockSpec(memory_space=pltpu.SMEM)
    packed = pl.BlockSpec((tok_rows, head_group * 3 * HD), lambda g: (0, g))
    totals = pl.BlockSpec((1, head_group, tok_rows), lambda g: (g, 0, 0))
    heads = pl.BlockSpec((tok_rows, head_group * HD), lambda g: (0, g))
    return scalars, packed, totals, heads


def attend_forward(packed, slopes, segments):
    tok_rows, width = packed.shape
    heads_here = width // (3 * HD)
    groups = heads_here // head_group
    scalars, packed_spec, totals, heads = attend_specs(tok_rows)
    return pl.pallas_call(
        forward_body,
        grid=(groups,),
        in_specs=[scalars, scalars, packed_spec],
        out_specs=[heads, totals],
        out_shape=[
            jax.ShapeDtypeStruct((tok_rows, heads_here * HD), jnp.bfloat16),
            jax.ShapeDtypeStruct((groups, head_group, tok_rows), jnp.float32),
        ],
        compiler_params=pltpu.CompilerParams(vmem_limit_bytes=40 * 2**20),
        cost_estimate=pl.CostEstimate(
            flops=4 * heads_here * tok_rows * tok_rows * HD,
            bytes_accessed=2 * tok_rows * width * 2,
            transcendentals=heads_here * tok_rows * tok_rows,
        ),
    )(segments, slopes, packed)


def attend_backward(packed, slopes, segments, log_totals, grad_attended):
    tok_rows, width = packed.shape
    heads_here = width // (3 * HD)
    scalars, packed_spec, totals, heads = attend_specs(tok_rows)
    return pl.pallas_call(
        backward_body,
        grid=(heads_here // head_group,),
        in_specs=[scalars, scalars, packed_spec, totals, heads],
        out_specs=packed_spec,
        out_shape=jax.ShapeDtypeStruct((tok_rows, width), jnp.bfloat16),
        scratch_shapes=[
            pltpu.VMEM((tok_rows, HD), jnp.float32),
            pltpu.VMEM((tok_rows, HD), jnp.float32),
        ],
        compiler_params=pltpu.CompilerParams(vmem_limit_bytes=40 * 2**20),
        cost_estimate=pl.CostEstimate(
            flops=10 * heads_here * tok_rows * tok_rows * HD,
            bytes_accessed=3 * tok_rows * width * 2,
            transcendentals=heads_here * tok_rows * tok_rows,
        ),
    )(segments, slopes, packed, log_totals, grad_attended)


def exchange_body(scatter, axis, devices, *refs):
    count = len(scatter)
    sources, results = refs[:count], refs[count : 2 * count]
    local_sem, send_sem, recv_sem = refs[2 * count :]
    me = lax.axis_index(axis)

    barrier = pltpu.get_barrier_semaphore()

    def greet(step, carry):
        peer = lax.rem(me + step, devices)
        pl.semaphore_signal(
            barrier, inc=1, device_id={axis: peer}, device_id_type=pl.DeviceIdType.MESH
        )
        return carry

    lax.fori_loop(1, devices, greet, 0)
    pl.semaphore_wait(barrier, devices - 1)

    def block_of(item, owner):
        return sources[item].at[owner] if scatter[item] else sources[item]

    def copy_to(item, step):
        peer = lax.rem(me + step, devices)
        return pltpu.make_async_remote_copy(
            src_ref=block_of(item, peer),
            dst_ref=results[item].at[me],
            send_sem=send_sem.at[item, step],
            recv_sem=recv_sem.at[item, step],
            device_id={axis: peer},
            device_id_type=pl.DeviceIdType.MESH,
        )

    def own_copy(item):
        return pltpu.make_async_copy(
            block_of(item, me), results[item].at[me], local_sem.at[item]
        )

    def start(step, carry):
        for item in range(count):
            copy_to(item, step).start()
        return carry

    def finish(step, carry):
        for item in range(count):
            copy_to(item, step).wait()
        return carry

    lax.fori_loop(1, devices, start, 0)
    for item in range(count):
        own_copy(item).start()
    for item in range(count):
        own_copy(item).wait()
    lax.fori_loop(1, devices, finish, 0)


def exchange(sources, scatter, axis, call_id):
    devices = lax.axis_size(axis)
    count = len(sources)
    shapes = [item.shape[1:] if apart else item.shape for apart, item in zip(scatter, sources)]
    size = sum(devices * rows * width * 2 for rows, width in shapes)
    return pl.pallas_call(
        partial(exchange_body, scatter, axis, devices),
        in_specs=[pl.BlockSpec(memory_space=pl.ANY)] * count,
        out_specs=[pl.BlockSpec(memory_space=pl.ANY)] * count,
        out_shape=[
            jax.ShapeDtypeStruct((devices, *shape), item.dtype)
            for shape, item in zip(shapes, sources)
        ],
        scratch_shapes=[
            pltpu.SemaphoreType.DMA((count,)),
            pltpu.SemaphoreType.DMA((count, devices)),
            pltpu.SemaphoreType.DMA((count, devices)),
        ],
        compiler_params=pltpu.CompilerParams(collective_id=call_id, has_side_effects=True),
        cost_estimate=pl.CostEstimate(flops=0, bytes_accessed=20 * size, transcendentals=0),
    )(*sources)


def gather_body(count, devices, *refs):
    sources, results = refs[:count], refs[count : 2 * count]
    local_sem, send_sem, recv_sem = refs[2 * count :]
    me = lax.axis_index("wide")
    beside = me + 1 - 2 * lax.rem(me, 2)
    steps = devices // 2

    barrier = pltpu.get_barrier_semaphore()

    def signal(peer):
        pl.semaphore_signal(
            barrier, inc=1, device_id={"wide": peer}, device_id_type=pl.DeviceIdType.MESH
        )

    def greet(step, carry):
        signal(lax.rem(me + 2 * step, devices))
        return carry

    lax.fori_loop(1, steps, greet, 0)
    signal(beside)
    pl.semaphore_wait(barrier, steps)

    def copy(item, source, slot, peer, index):
        return pltpu.make_async_remote_copy(
            src_ref=source,
            dst_ref=results[item].at[slot],
            send_sem=send_sem.at[item, index],
            recv_sem=recv_sem.at[item, index],
            device_id={"wide": peer},
            device_id_type=pl.DeviceIdType.MESH,
        )

    def copy_to(item, step):
        peer = lax.rem(me + 2 * step, devices)
        return copy(item, sources[item], me, peer, step)

    def pass_on(item, step):
        slot = lax.rem(me + devices - 2 * step, devices)
        return copy(item, results[item].at[slot], slot, beside, steps + step)

    def start(step, carry):
        for item in range(count):
            copy_to(item, step).start()
        return carry

    def forward(step, carry):
        for item in range(count):
            copy_to(item, step).wait_recv()
            pass_on(item, step).start()
        return carry

    def finish(step, carry):
        for item in range(count):
            copy_to(item, step).wait_send()
            pass_on(item, step).wait()
        return carry

    lax.fori_loop(1, steps, start, 0)
    for item in range(count):
        copy(item, sources[item], me, beside, 0).start()
    for item in range(count):
        own = pltpu.make_async_copy(sources[item], results[item].at[me], local_sem.at[item])
        own.start()
        own.wait()
    lax.fori_loop(1, steps, forward, 0)
    for item in range(count):
        copy(item, sources[item], me, beside, 0).wait()
    lax.fori_loop(1, steps, finish, 0)


def gather_rows(sources, call_id):
    devices = lax.axis_size("wide")
    count = len(sources)
    size = sum(2 * devices * item.size for item in sources)
    gathered = pl.pallas_call(
        partial(gather_body, count, devices),
        in_specs=[pl.BlockSpec(memory_space=pl.ANY)] * count,
        out_specs=[pl.BlockSpec(memory_space=pl.ANY)] * count,
        out_shape=[jax.ShapeDtypeStruct((devices, *item.shape), item.dtype) for item in sources],
        scratch_shapes=[
            pltpu.SemaphoreType.DMA((count,)),
            pltpu.SemaphoreType.DMA((count, devices)),
            pltpu.SemaphoreType.DMA((count, devices)),
        ],
        compiler_params=pltpu.CompilerParams(collective_id=call_id, has_side_effects=True),
        cost_estimate=pl.CostEstimate(flops=0, bytes_accessed=10 * size, transcendentals=0),
    )(*sources)
    return [item.reshape(-1, item.shape[-1]) for item in gathered]


def scatter_sums(sources, call_id, whole=()):
    devices = lax.axis_size("wide")
    blocks = [item.reshape(devices, -1, item.shape[-1]) for item in sources]
    scatter = (True,) * len(blocks) + (False,) * len(whole)
    parts = exchange([*blocks, *whole], scatter, "wide", call_id)
    return [jnp.sum(item.astype(jnp.float32), axis=0) for item in parts]


def local(
    tokens,
    segments,
    first_gain,
    first_shift,
    qkv_weight,
    qv_bias,
    dense_weight,
    dense_bias,
    second_gain,
    second_shift,
    up_weight,
    up_bias,
    down_weight,
    down_bias,
    cotangent,
):
    tok_rows, local_width = tokens.shape
    col_start = lax.axis_index("narrow") * local_width
    heads_here = qv_bias.shape[0] // (2 * HD)
    head_first = lax.axis_index("narrow") * heads_here
    slopes = 2.0 ** (-8.0 * (head_first + jnp.arange(heads_here) + 1).astype(jnp.float32) / H)
    out_rows = dense_weight.shape[1]
    vectors = jnp.stack([first_gain, first_shift, dense_bias, second_gain, second_shift])
    vectors = jnp.pad(vectors, ((0, 11), (0, 0)))
    joined = lax.all_gather(
        jnp.concatenate([tokens, dense_weight.T, vectors], axis=0), "narrow", axis=1, tiled=True
    )
    full_tokens = joined[:tok_rows]
    dense_block = joined[tok_rows : tok_rows + out_rows]
    gain_one, shift_one, bias_dense, gain_two, shift_two = (
        joined[tok_rows + out_rows + item].astype(jnp.float32) for item in range(5)
    )
    qkv_full, up_full = gather_rows([qkv_weight, up_weight], 0)
    grad_out = lax.all_gather(cotangent, "narrow", axis=1, tiled=True)
    inputs = full_tokens.astype(jnp.float32)
    normed_one, hat_one, inv_one = normalize(inputs, gain_one, shift_one)
    act_one = normed_one.astype(jnp.bfloat16)
    bias_pair = qv_bias.astype(jnp.float32).reshape(heads_here, 2, HD)
    full_bias = jnp.stack(
        [bias_pair[:, 0], jnp.zeros_like(bias_pair[:, 0]), bias_pair[:, 1]], axis=1
    ).reshape(-1)
    packed = (
        jnp.dot(act_one, qkv_full, preferred_element_type=jnp.float32) + full_bias[None]
    ).astype(jnp.bfloat16)
    attended, log_totals = attend_forward(packed, slopes, segments)
    half_rows = tok_rows // 2
    spans = [slice(0, half_rows), slice(half_rows, tok_rows)]
    attended_halves = [
        lax.all_gather(attended[span], "narrow", axis=1, tiled=True) for span in spans
    ]
    dense_block, grad_out = lax.optimization_barrier((dense_block, grad_out))
    dense_rows, down_rows = gather_rows([dense_block, down_weight.T], 1)
    kept = []
    grad_parts = []
    for span, attended_half in zip(spans, attended_halves):
        if grad_parts:
            attended_half, _ = lax.optimization_barrier((attended_half, grad_parts[0]))
        mixed = contract(attended_half, dense_rows, 1, 1)
        residual = inputs[span] + (mixed + bias_dense)
        normed_two, hat_two, inv_two = normalize(residual, gain_two, shift_two)
        act_two = normed_two.astype(jnp.bfloat16)
        pre_act = jnp.dot(act_two, up_full, preferred_element_type=jnp.float32) + up_bias.astype(
            jnp.float32
        )
        hidden = jax.nn.gelu(pre_act, approximate=True).astype(jnp.bfloat16)
        grad_hidden = jnp.dot(grad_out[span], down_rows, preferred_element_type=jnp.float32)
        _, gelu_back = jax.vjp(partial(jax.nn.gelu, approximate=True), pre_act)
        grad_pre = gelu_back(grad_hidden)[0].astype(jnp.bfloat16)
        grad_parts.append(contract(grad_pre, up_full, 1, 1).astype(jnp.bfloat16))
        kept.append(
            (own_columns(residual, col_start, local_width), hat_two, inv_two, act_two, hidden, grad_pre)
        )
    grad_twos = [lax.psum(grad_parts[0], "narrow")]
    grad_parts[1], grad_twos[0] = lax.optimization_barrier((grad_parts[1], grad_twos[0]))
    grad_twos.append(lax.psum(grad_parts[1], "narrow"))
    own_residual, act_two, hidden, grad_pre = (
        jnp.concatenate([kept[0][item], kept[1][item]], axis=0) for item in (0, 3, 4, 5)
    )
    mlp_part = contract(hidden, down_rows, 1, 1).astype(jnp.bfloat16)
    mlp_part, grad_twos[1] = lax.optimization_barrier((mlp_part, grad_twos[1]))
    mlp_out = lax.psum_scatter(
        mlp_part,
        "narrow",
        scatter_dimension=1,
        tiled=True,
    ).astype(jnp.float32)
    output = (
        own_residual + (mlp_out + down_bias.astype(jnp.float32))
    ).astype(jnp.bfloat16)
    down_bias_grad = jnp.sum(cotangent.astype(jnp.float32), axis=0)
    up_bias_grad = jnp.sum(grad_pre.astype(jnp.float32), axis=0)
    grad_down = contract(grad_out, hidden, 0, 0).astype(jnp.bfloat16)
    grad_up = contract(act_two, grad_pre, 0, 0).astype(jnp.bfloat16)
    up_weight_grad, down_rows_grad = scatter_sums([grad_up, grad_down], 2)
    grad_twos[1], up_weight_grad, down_rows_grad = lax.optimization_barrier(
        (grad_twos[1], up_weight_grad, down_rows_grad)
    )
    dense_own = own_columns(dense_rows, col_start, local_width)
    back = []
    sums = []
    for span, grad_two, (_, hat_two, inv_two, _, _, _) in zip(spans, grad_twos, kept):
        grad_act_two = grad_two.astype(jnp.float32)
        grad_residual = grad_out[span].astype(jnp.float32) + norm_backward(
            grad_act_two, gain_two, hat_two, inv_two
        )
        grad_branch = grad_residual.astype(jnp.bfloat16)
        sums.append(
            (
                jnp.sum(grad_act_two * hat_two, axis=0),
                jnp.sum(grad_act_two, axis=0),
                jnp.sum(grad_branch.astype(jnp.float32), axis=0),
            )
        )
        grad_attended = jnp.dot(
            grad_branch, dense_own, preferred_element_type=jnp.float32
        ).astype(jnp.bfloat16)
        back.append(
            (own_columns(grad_residual, col_start, local_width), grad_branch, grad_attended)
        )
    own_grad_residual, grad_branch, grad_attended = (
        jnp.concatenate(pair, axis=0) for pair in zip(*back)
    )
    second_gain_grad, second_shift_grad, dense_bias_grad = (
        own_columns(low + high, col_start, local_width) for low, high in zip(*sums)
    )
    grad_packed = attend_backward(packed, slopes, segments, log_totals, grad_attended)
    column_sums = jnp.sum(grad_packed.astype(jnp.float32), axis=0).reshape(heads_here, 3, HD)
    qv_bias_grad = jnp.stack([column_sums[:, 0], column_sums[:, 2]], axis=1).reshape(-1)
    grad_one_part = contract(grad_packed, qkv_full, 1, 1)
    grad_act_one = lax.psum_scatter(
        grad_one_part.astype(jnp.bfloat16), "narrow", scatter_dimension=1, tiled=True
    ).astype(jnp.float32)
    scaled_part = grad_one_part * gain_one
    row_sums = jnp.stack([jnp.sum(scaled_part, axis=1), jnp.sum(scaled_part * hat_one, axis=1)])
    feature_sums = jnp.stack(
        [jnp.sum(grad_one_part * hat_one, axis=0), jnp.sum(grad_one_part, axis=0)]
    )
    lines = jnp.concatenate([row_sums.reshape(-1, 128), feature_sums.reshape(-1, 128)], axis=0)
    (line_parts,) = exchange([lines], (False,), "narrow", 4)
    flat_sums = jnp.sum(line_parts, axis=0).reshape(-1)
    sum_plain, sum_hat = flat_sums[: 2 * tok_rows].reshape(2, tok_rows)
    gain_part, shift_part = flat_sums[2 * tok_rows :].reshape(2, -1)
    grad_qkv = contract(act_one, grad_packed, 0, 0).astype(jnp.bfloat16)
    grad_dense = contract(grad_branch, attended, 0, 0).astype(jnp.bfloat16)
    small = (
        own_columns(gain_part, col_start, local_width),
        own_columns(shift_part, col_start, local_width),
        qv_bias_grad,
        dense_bias_grad,
        second_gain_grad,
        second_shift_grad,
        up_bias_grad,
        down_bias_grad,
    )
    qkv_weight_grad, dense_rows_grad, small_sums = scatter_sums(
        [grad_qkv, grad_dense], 3, [jnp.concatenate(small).reshape(-1, 128)]
    )
    small_sums = small_sums.reshape(-1)
    bounds = [0]
    for item in small:
        bounds.append(bounds[-1] + item.shape[0])
    (
        first_gain_grad,
        first_shift_grad,
        qv_bias_grad,
        dense_bias_grad,
        second_gain_grad,
        second_shift_grad,
        up_bias_grad,
        down_bias_grad,
    ) = (small_sums[low:high] for low, high in zip(bounds, bounds[1:]))
    hat_local = own_columns(hat_one, col_start, local_width)
    scaled = grad_act_one * first_gain.astype(jnp.float32)
    full_width = local_width * lax.axis_size("narrow")
    grad_norm_one = inv_one * (
        scaled - sum_plain[:, None] / full_width - hat_local * sum_hat[:, None] / full_width
    )
    token_grad = (own_grad_residual + grad_norm_one).astype(
        jnp.bfloat16
    )
    dense_weight_grad = dense_rows_grad.T
    down_weight_grad = down_rows_grad.T
    return (
        output,
        token_grad,
        first_gain_grad,
        first_shift_grad,
        qkv_weight_grad,
        qv_bias_grad,
        dense_weight_grad,
        dense_bias_grad,
        second_gain_grad,
        second_shift_grad,
        up_weight_grad,
        up_bias_grad,
        down_weight_grad,
        down_bias_grad,
    )


def solution(mesh):
    in_specs = (
        P("wide", "narrow"),
        P("wide"),
        P("narrow"),
        P("narrow"),
        P("wide", "narrow"),
        P("narrow"),
        P("narrow", "wide"),
        P("narrow"),
        P("narrow"),
        P("narrow"),
        P("wide", "narrow"),
        P("narrow"),
        P("narrow", "wide"),
        P("narrow"),
        P("wide", "narrow"),
    )
    out_specs = (
        P("wide", "narrow"),
        P("wide", "narrow"),
        P("narrow"),
        P("narrow"),
        P("wide", "narrow"),
        P("narrow"),
        P("narrow", "wide"),
        P("narrow"),
        P("narrow"),
        P("narrow"),
        P("wide", "narrow"),
        P("narrow"),
        P("narrow", "wide"),
        P("narrow"),
    )
    return jax.shard_map(local, mesh=mesh, in_specs=in_specs, out_specs=out_specs, check_vma=False)
```
